32 devices in a mesh: seq: 8 (over y, x, core), chan: 4 (over z).
Axes of the slice: x: 2, y: 2, z: 4, core: 2. Of those that a mesh axis runs over, the one named last changes fastest.
Arguments:
- features: bfloat16 [3, 2, 8192, 1024], P(None, None, 'chan', 'seq'), may hold values from -6 to 6
- offsets: int32 [2], replicated, may hold values from 0 to 511
- tokens: int32 [2, 4], replicated, may hold values from 0 to 511
- decay_rate: float32 [16, 8192], P(None, 'chan'), may hold values from 0 to 1
- residue: float32 [16, 8192], P(None, 'chan'), may hold values from -1 to 1
- skip_weight: float32 [8192], P('chan'), may hold values from -3 to 3
- embedding: bfloat16 [512, 8192], P(None, 'seq'), may hold values from -12 to 12
- norm_gain: float32 [8192], P('seq'), may hold values from 0.1 to 1.9
- dec_weight: bfloat16 [3, 8192, 8192], P(None, 'seq', 'chan'), may hold values from -0.09375 to 0.09375
- out_weight: bfloat16 [8192, 8192], P('chan', 'seq'), may hold values from -0.09375 to 0.09375
Outputs:
- mixed: bfloat16 [2, 8192, 1024], P(None, 'chan', 'seq')
- decoded: bfloat16 [2, 4, 8192], P(None, None, ('seq', 'chan'))
The draws below stay inside these ranges and needn't reach their ends.
All inputs are finite; a program needn't handle non-finite values.
Results may differ from the reference program's by a relative error of at most 0.0082.
Values may be sent and summed in bfloat16 or wider, within the bound.
A program may use at most 128 MiB of HBM per device.

```python
import math
import jax
import jax.numpy as jnp
import numpy as np
from jax import lax

D = 8192
MODES = 16
VOCAB = 512
BATCH = 2
STEPS = 4
WINDOW = 1024


def rate_and_residue(key):
    base = jax.random.fold_in(key, 7)
    pick_key, slow_key, fast_key, res_key = jax.random.split(base, 4)
    slow_share = 0.5
    picked = jax.random.uniform(pick_key, (MODES, D), jnp.float32) < slow_share
    slow_rate = jnp.exp(jax.random.uniform(slow_key, (MODES, D), jnp.float32, math.log(0.2 / WINDOW), math.log(2.0 / WINDOW)))
    fast_rate = jnp.exp(jax.random.uniform(fast_key, (MODES, D), jnp.float32, math.log(2.0 / WINDOW), math.log(1.0 / 30.0)))
    rates = jnp.where(picked, slow_rate, fast_rate)
    noise = jnp.clip(jax.random.normal(res_key, (MODES, D), jnp.float32), -4.0, 4.0)
    residues = noise * jnp.sqrt(2.0 * rates / MODES)
    return (rates, residues)


def draw_decay_rate(key, part):
    return rate_and_residue(key)[0]


def draw_residue(key, part):
    return rate_and_residue(key)[1]


def draw_embedding(key, part):
    base = jax.random.fold_in(key, 19)
    column = jnp.arange(D, dtype=jnp.float32) / D
    values = jnp.clip(jax.random.normal(base, (VOCAB, D), jnp.float32), -4.0, 4.0) * (1.0 + 2.0 * column)
    return values.astype(jnp.bfloat16)


def touch_ends(values, key, low, top_value):
    shape = values.shape
    index_at = [jax.random.randint(jax.random.fold_in(key, axis), (), 0, shape[axis]) for axis in range(len(shape))]
    values = values.at[tuple(index_at)].set(low)
    longest = shape.index(max(shape))
    index_at[longest] = (index_at[longest] + 1) % shape[longest]
    return values.at[tuple(index_at)].set(top_value)


def strengthened(result, stream_key, source, target, parts, factor):
    def block_of(dim):
        return (jnp.arange(result.shape[dim]) // (result.shape[dim] // parts)).reshape((-1,) + (1,) * (result.ndim - 1 - dim))

    first = jax.random.permutation(stream_key, parts)[block_of(target)]
    far = (block_of(target) + parts // 2) % parts
    return jnp.where((block_of(source) == first) | (block_of(source) == far), factor * result, result)


def steps_of(stream_key, shape, cuts, smallest, high):
    factor_of, own = 1.0, jax.random.fold_in(stream_key, 6)
    for axis_at, blocks in cuts:
        draws = jnp.exp(jax.random.uniform(jax.random.fold_in(own, axis_at), (blocks,), jnp.float32, smallest / len(cuts), high / len(cuts)))
        factor_of = factor_of * jnp.repeat(draws, shape[axis_at] // blocks).reshape([-1 if axis == axis_at else 1 for axis in range(len(shape))])
    return factor_of


def rank_bounds(number_of, skew):
    portions = [(1 << 20) // math.isqrt(rank ** skew) + 1 for rank in range(1, number_of + 1)]
    spread = 1 + sum(portions) // (1 << 30)
    return np.cumsum(np.array([max(1, weight // spread) for weight in portions]))


def ranked(own_key, extent, number_of, skew):
    grid = rank_bounds(number_of, skew)
    lot = jax.random.randint(jax.random.fold_in(own_key, 1), extent, 0, int(grid[number_of - 1]))
    standing = jnp.searchsorted(jnp.asarray(grid, jnp.int32), lot, side="right")
    return jax.random.permutation(jax.random.fold_in(own_key, 2), number_of)[standing].astype(jnp.int32)


def gaussian(stream_key, shape, spread, limit, pieces=(), kind=jnp.bfloat16):
    entries = spread * jax.random.normal(stream_key, shape, jnp.float32)
    if pieces:
        entries = entries * steps_of(stream_key, shape, pieces, -0.22, 0.18)
    return jnp.clip(entries, -limit, limit).astype(kind)


def heavy_noise(own_key, dims, spread, limit, pieces, heavy, held_as=jnp.bfloat16):
    drawn = spread * jax.random.normal(own_key, dims, jnp.float32)
    if pieces:
        drawn = drawn * steps_of(own_key, dims, pieces, -0.22, 0.18)
    return jnp.clip(strengthened(drawn, jax.random.fold_in(own_key, 3), *heavy), -limit, limit).astype(held_as)


def setup_inputs(seed: int = 0) -> dict:
    splits = jax.random.split(jax.random.key(seed), 11)
    features = gaussian(splits[0], (3, BATCH, D, WINDOW), 1.0, 6.0, ((2, 4), (3, 8)))
    offsets = jax.random.randint(splits[1], (BATCH,), 0, WINDOW // 2).astype(jnp.int32)
    tokens = touch_ends(ranked(splits[2], (BATCH, STEPS), VOCAB, 2), jax.random.fold_in(splits[2], 3), 0, VOCAB - 1).astype(jnp.int32)
    decay_rate = draw_decay_rate(jax.random.fold_in(splits[10], 71), 0)
    residue = draw_residue(jax.random.fold_in(splits[10], 71), 0)
    skip_weight = gaussian(splits[5], (D,), 0.5, 3.0, ((0, 4),), jnp.float32)
    embedding = draw_embedding(jax.random.fold_in(splits[10], 71), 0)
    norm_gain = jnp.clip(1.0 + 0.18 * jax.random.normal(splits[7], (D,), jnp.float32), 0.1, 1.9)
    dec_weight = heavy_noise(splits[8], (3, D, D), D ** -0.5, 0.09375, ((1, 8), (2, 4)), (1, 2, 8, 2.0))
    out_weight = heavy_noise(splits[9], (D, D), D ** -0.5, 0.09375, ((0, 4), (1, 8)), (0, 1, 8, 2.0))
    return {"features": features, "offsets": offsets, "tokens": tokens, "decay_rate": decay_rate, "residue": residue, "skip_weight": skip_weight, "embedding": embedding, "norm_gain": norm_gain, "dec_weight": dec_weight, "out_weight": out_weight}


def reference(features, offsets, tokens, decay_rate, residue, skip_weight, embedding, norm_gain, dec_weight, out_weight):
    highest = lax.Precision.HIGHEST
    query = features[0]
    keys_in = features[1]
    values_in = features[2]
    positions = jnp.arange(WINDOW, dtype=jnp.int32)
    live = positions[None, :] >= offsets[:, None].astype(jnp.int32)
    product = jnp.where(live[:, None, :], keys_in.astype(jnp.float32) * values_in.astype(jnp.float32), jnp.float32(0.0)).astype(jnp.bfloat16)
    width = 128
    nblocks = D // width

    def one_block(packed):
        sig_block, query_block, rate_block, res_block, skip_block = packed
        lag_pos = jnp.arange(WINDOW, dtype=jnp.float32)
        filt = lax.optimization_barrier(jnp.sum(res_block[:, :, None] * jnp.exp(-rate_block[:, :, None] * lag_pos), axis=0))
        signal = sig_block.astype(jnp.float32)
        length = 2 * WINDOW
        spectrum = jnp.fft.rfft(signal, length) * jnp.fft.rfft(filt, length)[None]
        conv = jnp.fft.irfft(spectrum, length)[..., :WINDOW]
        conv = conv + skip_block[None, :, None] * signal
        mixed_block = (query_block.astype(jnp.float32) * conv).astype(jnp.bfloat16)
        weights = jnp.exp(-rate_block[:, :, None] * (WINDOW - 1 - lag_pos))
        state_block = jnp.einsum('mcl,bcl->bmc', weights, signal, precision=highest)
        return (mixed_block, state_block)
    packed = (product.reshape(BATCH, nblocks, width, WINDOW).transpose(1, 0, 2, 3), query.reshape(BATCH, nblocks, width, WINDOW).transpose(1, 0, 2, 3), decay_rate.reshape(MODES, nblocks, width).transpose(1, 0, 2), residue.reshape(MODES, nblocks, width).transpose(1, 0, 2), skip_weight.reshape(nblocks, width))
    mixed_blocks, state_blocks = lax.map(one_block, packed)
    mixed = mixed_blocks.transpose(1, 0, 2, 3).reshape(BATCH, D, WINDOW)
    state = state_blocks.transpose(1, 2, 0, 3).reshape(BATCH, MODES, D)
    embedded = jnp.take(embedding, tokens, axis=0).astype(jnp.float32)
    mean_sq = lax.optimization_barrier(jnp.sum(embedded * embedded, axis=-1, keepdims=True)) / D
    normed = (embedded * lax.rsqrt(mean_sq + 1e-05) * norm_gain).astype(jnp.bfloat16)
    proj = jnp.einsum('bsd,idc->ibsc', normed.astype(jnp.float32), dec_weight.astype(jnp.float32)).astype(jnp.bfloat16)
    decay = jnp.exp(-decay_rate)
    running = state
    outputs = []
    for step in range(STEPS):
        rounded = lax.optimization_barrier((proj[1, :, step].astype(jnp.float32) * proj[2, :, step].astype(jnp.float32)).astype(jnp.bfloat16))
        mixed_in = rounded.astype(jnp.float32)
        running = decay[None] * running + mixed_in[:, None, :]
        conv_step = lax.optimization_barrier(jnp.sum(residue[None] * running, axis=1)) + skip_weight[None] * mixed_in
        outputs.append((proj[0, :, step].astype(jnp.float32) * conv_step).astype(jnp.bfloat16))
    decode_mix = jnp.stack(outputs, axis=1)
    decoded = jnp.dot(decode_mix.reshape(BATCH * STEPS, D), out_weight, preferred_element_type=jnp.float32)
    decoded = decoded.astype(jnp.bfloat16).reshape(BATCH, STEPS, D)
    return (mixed, decoded)
```

```python
import functools

import jax
import jax.numpy as jnp
from jax import lax
from jax.experimental import pallas as pl
from jax.experimental.pallas import tpu as pltpu
from jax.sharding import PartitionSpec as P

LANES = 128
F32 = jnp.float32
BF16 = jnp.bfloat16
VMEM = pl.BlockSpec(memory_space=pltpu.VMEM)
ANY = pl.BlockSpec(memory_space=pl.ANY)
SMEM = pl.BlockSpec(memory_space=pltpu.SMEM)
LIMIT = 50 * 2**20


def first_kernel(
    seq_count, steps,
    feat, offsets, tokens, par, embedding, gain, weight,
    ut, send,
    kv, held, kv_sem, w_sem,
):
    _, batch, chans, length = feat.shape
    groups = chans // LANES
    modes = (par.shape[0] - 1) // 2
    per = max(1, groups // seq_count)
    kv_copy = pltpu.make_async_copy(feat.at[pl.ds(1, 2)], kv, kv_sem)
    kv_copy.start()
    w_copies = [
        pltpu.make_async_copy(weight.at[i], held.at[i], w_sem.at[i]) for i in range(3)
    ]
    for copy in w_copies:
        copy.start()

    count = tokens.shape[0]
    vocab = embedding.shape[0]
    hot = (tokens[...] == lax.broadcasted_iota(jnp.int32, (count, vocab), 1)).astype(F32).astype(BF16)
    rows = jnp.dot(hot, embedding[...], preferred_element_type=F32)
    squares = jnp.broadcast_to(jnp.sum(rows * rows, axis=1, keepdims=True), (count, LANES))
    scaled = rows * gain[...]
    high = scaled.astype(BF16)
    low = (scaled - high.astype(F32)).astype(BF16)
    both = jnp.concatenate([high.astype(F32), low.astype(F32)], axis=0).astype(BF16)
    base = batch * modes
    for j in range(groups // per):
        send[j, pl.ds((base + 3 * count) * per, count), :] = squares

    kv_copy.wait()
    start = lax.axis_index("seq") * length
    place = start + lax.broadcasted_iota(jnp.int32, (LANES, length), 1)

    def turn(g, carry):
        at = pl.ds(pl.multiple_of(g * LANES, LANES), LANES)
        for b in range(batch):
            product = kv[0, b, at, :].astype(F32) * kv[1, b, at, :].astype(F32)
            signal = jnp.where(place >= offsets[b], product, 0.0).astype(BF16).astype(F32)
            ut[b, pl.ds(g, length, stride=groups), :] = signal.T
        return carry

    lax.fori_loop(0, groups, turn, 0)

    for h in range(groups // 8):
        decay = [jnp.exp(-par[m, 8 * h : 8 * h + 8, :]) for m in range(modes)]

        def step(t, state):
            at = pl.ds(pl.multiple_of(t * groups + 8 * h, 8), 8)
            now = [ut[b, at, :] for b in range(batch)]
            return tuple(
                decay[m] * state[b * modes + m] + now[b]
                for b in range(batch)
                for m in range(modes)
            )

        zero = jnp.zeros((8, LANES), F32)
        ends = lax.fori_loop(0, length, step, (zero,) * base, unroll=4)
        for r in range(base):
            for g in range(8):
                j, at = divmod(8 * h + g, per)
                send[j, r * per + at, :] = ends[r][g]

    for i in range(3):
        w_copies[i].wait()
        for c in range(0, chans, 512):
            term = jnp.dot(both, held[i, :, c : c + 512], preferred_element_type=F32)
            term = term[:count] + term[count:]
            for g in range(4):
                j, at = divmod(c // LANES + g, per)
                first = (base + i * count) * per + at
                send[j, pl.ds(first, count, stride=per), :] = term[:, g * LANES : (g + 1) * LANES]


def exchange(mine, chan, seq_count, share, source, target, send_sem, recv_sem):
    target[mine] = source[lax.div(mine, share)]
    copies = []
    for d in range(1, seq_count):
        other = lax.rem(mine + d, seq_count)
        copies.append(
            pltpu.make_async_remote_copy(
                src_ref=source.at[lax.div(other, share)],
                dst_ref=target.at[mine],
                send_sem=send_sem.at[d - 1],
                recv_sem=recv_sem.at[d - 1],
                device_id=(other, chan),
                device_id_type=pl.DeviceIdType.MESH,
            )
        )
    for copy in copies:
        copy.start()
    return copies


def middle_kernel(
    seq_count, chan_count, batch, steps, modes, length, width,
    send, own, out_weight,
    carried, decoded,
    got, back, got_back, rows, spread, proj, scale, mix, part, got_part, held, w_sem,
    send_a, recv_a, send_b, recv_b, send_c, recv_c,
):
    mine, chan = lax.axis_index("seq"), lax.axis_index("chan")
    per = own.shape[0] // (2 * modes + 1)
    slots = send.shape[0]
    share = seq_count // slots
    count = batch * steps
    base = batch * modes
    block = modes * per
    w_copy = pltpu.make_async_copy(out_weight, held, w_sem)
    w_copy.start()
    barrier = pltpu.get_barrier_semaphore()
    for d in range(1, seq_count):
        pl.semaphore_signal(
            barrier, inc=1, device_id=(lax.rem(mine + d, seq_count), chan),
            device_id_type=pl.DeviceIdType.MESH,
        )
    for d in range(1, chan_count):
        pl.semaphore_signal(
            barrier, inc=1, device_id=(mine, lax.rem(chan + d, chan_count)),
            device_id_type=pl.DeviceIdType.MESH,
        )
    pl.semaphore_wait(barrier, seq_count + chan_count - 2)

    copies = exchange(mine, chan, seq_count, share, send, got, send_a, recv_a)
    rate = own[:block, :]
    decay = jnp.exp(-rate)
    power = jnp.exp(-rate * float(length))
    residue = own[block : 2 * block, :]
    skip = own[2 * block :, :]
    for copy in copies:
        copy.wait()

    state = []
    for b in range(batch):
        running = jnp.zeros((block, LANES), F32)
        for j in range(seq_count):
            back[j, b * block : (b + 1) * block, :] = running
            running = power * running + got[j, b * block : (b + 1) * block, :]
        state.append(running)

    first = base * per
    total = got[0, first : first + 3 * count * per, :]
    squares = got[0, first + 3 * count * per :, :]
    for j in range(1, seq_count):
        total = total + got[j, first : first + 3 * count * per, :]
        squares = squares + got[j, first + 3 * count * per :, :]
    proj[...] = total
    scale[...] = lax.rsqrt(squares / float(width) + 1e-05)

    def projected(i, token):
        at = (i * count + token) * per
        value = proj[at : at + per, :] * scale[token : token + 1, :]
        return value.astype(BF16).astype(F32)

    for b in range(batch):
        running = state[b]
        for s in range(steps):
            token = b * steps + s
            fed = (projected(1, token) * projected(2, token)).astype(BF16).astype(F32)
            for m in range(modes):
                spread[m * per : (m + 1) * per, :] = fed
            running = decay * running + spread[...]
            rows[...] = residue * running
            value = skip * fed
            for m in range(modes):
                value = value + rows[m * per : (m + 1) * per, :]
            value = (projected(0, token) * value).astype(BF16).astype(F32)
            at = first + token * per
            for j in range(seq_count):
                back[j, at : at + per, :] = value

    copies_back = exchange(mine, chan, seq_count, 1, back, got_back, send_b, recv_b)
    for copy in copies_back:
        copy.wait()
    for j in range(slots):
        for g in range(per):
            at = j * per + g
            mix[:, at * LANES : (at + 1) * LANES] = got_back[j * share, pl.ds(first + g, count, stride=per), :]
    w_copy.wait()
    piece = held.shape[1] // chan_count
    mixed = mix[...].astype(BF16)
    for c in range(chan_count):
        part[c] = jnp.dot(
            mixed, held[:, c * piece : (c + 1) * piece], preferred_element_type=F32
        )
    got_part[chan] = part[chan]
    sums = []
    for d in range(1, chan_count):
        other = lax.rem(chan + d, chan_count)
        sums.append(
            pltpu.make_async_remote_copy(
                src_ref=part.at[other],
                dst_ref=got_part.at[chan],
                send_sem=send_c.at[d - 1],
                recv_sem=recv_c.at[d - 1],
                device_id=(mine, other),
                device_id_type=pl.DeviceIdType.MESH,
            )
        )
    for copy in sums:
        copy.start()
    for j in range(slots):
        for r in range(base):
            carried[r, j * per : (j + 1) * per, :] = got_back[j * share, r * per : (r + 1) * per, :]
    for copy in sums:
        copy.wait()
    value = got_part[0]
    for c in range(1, chan_count):
        value = value + got_part[c]
    decoded[...] = value.astype(BF16)


def last_kernel(feat, ut, par, carried, mixed, query, conv, q_sem):
    _, batch, chans, length = feat.shape
    groups = chans // LANES
    modes = (par.shape[0] - 1) // 2
    q_copy = pltpu.make_async_copy(feat.at[0], query, q_sem)
    q_copy.start()
    for h in range(groups // 8):
        tile = slice(8 * h, 8 * h + 8)
        decay = [jnp.exp(-par[m, tile, :]) for m in range(modes)]
        residue = [par[modes + m, tile, :] for m in range(modes)]
        skip = par[2 * modes, tile, :]
        for b in range(batch):

            def step(t, state):
                at = pl.ds(pl.multiple_of(t * groups + 8 * h, 8), 8)
                now = ut[b, at, :]
                state = [decay[m] * state[m] + residue[m] * now for m in range(modes)]
                terms = list(state) + [skip * now]
                while len(terms) > 1:
                    pairs = [x + y for x, y in zip(terms[::2], terms[1::2])]
                    terms = pairs + terms[len(pairs) * 2 :]
                conv[b, at, :] = terms[0]
                return tuple(state)

            begin = tuple(residue[m] * carried[b * modes + m, tile, :] for m in range(modes))
            lax.fori_loop(0, length, step, begin, unroll=4)
    q_copy.wait()

    def turn(g, carry):
        at = pl.ds(pl.multiple_of(g * LANES, LANES), LANES)
        for b in range(batch):
            value = conv[b, pl.ds(g, length, stride=groups), :].T
            mixed[b, at, :] = (query[b, at, :].astype(F32) * value).astype(BF16)
        return carry

    lax.fori_loop(0, groups, turn, 0)


def body(
    features, offsets, tokens, decay_rate, residue, skip_weight,
    embedding, norm_gain, dec_weight, out_weight,
):
    seq_count, chan_count = lax.axis_size("seq"), lax.axis_size("chan")
    _, batch, chans, length = features.shape
    modes = decay_rate.shape[0]
    steps = tokens.shape[1]
    count = batch * steps
    groups = chans // LANES
    per = max(1, groups // seq_count)
    slots = groups // per
    depth = embedding.shape[1]
    base = batch * modes
    rows = (base + 3 * count) * per + count
    par = jnp.concatenate([decay_rate, residue, skip_weight[None]], axis=0)
    slot = lax.axis_index("seq") // (seq_count // slots)
    own = lax.dynamic_slice_in_dim(par, slot * per * LANES, per * LANES, 1)
    own = own.reshape((2 * modes + 1) * per, LANES)
    par = par.reshape(2 * modes + 1, groups, LANES)
    params = functools.partial(pltpu.CompilerParams, vmem_limit_bytes=LIMIT)

    ut, send = pl.pallas_call(
        functools.partial(first_kernel, seq_count, steps),
        out_shape=(
            jax.ShapeDtypeStruct((batch, length * groups, LANES), F32),
            jax.ShapeDtypeStruct((slots, rows, LANES), F32),
        ),
        in_specs=[ANY, SMEM, VMEM, VMEM, VMEM, VMEM, ANY],
        out_specs=(VMEM, VMEM),
        scratch_shapes=[
            pltpu.VMEM((2, batch, chans, length), BF16),
            pltpu.VMEM((3, depth, chans), BF16),
            pltpu.SemaphoreType.DMA,
            pltpu.SemaphoreType.DMA((3,)),
        ],
        compiler_params=params(),
        name="ends_and_projections",
    )(features, offsets, tokens.reshape(count, 1), par, embedding, norm_gain[None], dec_weight)

    out_width = out_weight.shape[1]
    back_rows = (base + count) * per
    carried, decoded = pl.pallas_call(
        functools.partial(
            middle_kernel, seq_count, chan_count, batch, steps, modes, length, depth * seq_count
        ),
        out_shape=(
            jax.ShapeDtypeStruct((base, groups, LANES), F32),
            jax.ShapeDtypeStruct((count, out_width // chan_count), BF16),
        ),
        in_specs=[VMEM, VMEM, ANY],
        out_specs=(VMEM, VMEM),
        scratch_shapes=[
            pltpu.VMEM((seq_count, rows, LANES), F32),
            pltpu.VMEM((seq_count, back_rows, LANES), F32),
            pltpu.VMEM((seq_count, back_rows, LANES), F32),
            pltpu.VMEM((modes * per, LANES), F32),
            pltpu.VMEM((modes * per, LANES), F32),
            pltpu.VMEM((3 * count * per, LANES), F32),
            pltpu.VMEM((count, LANES), F32),
            pltpu.VMEM((count, chans), F32),
            pltpu.VMEM((chan_count, count, out_width // chan_count), F32),
            pltpu.VMEM((chan_count, count, out_width // chan_count), F32),
            pltpu.VMEM(out_weight.shape, BF16),
            pltpu.SemaphoreType.DMA,
            pltpu.SemaphoreType.DMA((seq_count - 1,)),
            pltpu.SemaphoreType.DMA((seq_count - 1,)),
            pltpu.SemaphoreType.DMA((seq_count - 1,)),
            pltpu.SemaphoreType.DMA((seq_count - 1,)),
            pltpu.SemaphoreType.DMA((chan_count - 1,)),
            pltpu.SemaphoreType.DMA((chan_count - 1,)),
        ],
        compiler_params=params(collective_id=0, has_side_effects=True),
        name="exchange_and_decode",
    )(send, own, out_weight)

    mixed = pl.pallas_call(
        last_kernel,
        out_shape=jax.ShapeDtypeStruct((batch, chans, length), BF16),
        in_specs=[ANY, VMEM, VMEM, VMEM],
        out_specs=VMEM,
        scratch_shapes=[
            pltpu.VMEM((batch, chans, length), BF16),
            pltpu.VMEM((batch, length * groups, LANES), F32),
            pltpu.SemaphoreType.DMA,
        ],
        compiler_params=params(),
        name="conv_and_gate",
    )(features, ut, par, carried)
    return mixed, decoded.reshape(batch, steps, -1)


def solution(mesh):
    placed = (
        P(None, None, "chan", "seq"),
        P(),
        P(),
        P(None, "chan"),
        P(None, "chan"),
        P("chan"),
        P(None, "seq"),
        P("seq"),
        P(None, "seq", "chan"),
        P("chan", "seq"),
    )
    return jax.shard_map(
        body,
        mesh=mesh,
        in_specs=placed,
        out_specs=(P(None, "chan", "seq"), P(None, None, ("seq", "chan"))),
        check_vma=False,
    )
```

```python
import functools

import jax
import jax.numpy as jnp
from jax import lax
from jax.experimental import pallas as pl
from jax.experimental.pallas import tpu as pltpu
from jax.sharding import PartitionSpec as P

LANES = 128
F32 = jnp.float32
BF16 = jnp.bfloat16
VMEM = pl.BlockSpec(memory_space=pltpu.VMEM)
ANY = pl.BlockSpec(memory_space=pl.ANY)
SMEM = pl.BlockSpec(memory_space=pltpu.SMEM)
LIMIT = 56 * 2**20


def exchange(mine, chan, count, source, target, send_sem, recv_sem, axis="seq"):
    here = mine if axis == "seq" else chan
    copies = []
    for d in range(1, count):
        other = lax.rem(here + d, count)
        copies.append(
            pltpu.make_async_remote_copy(
                src_ref=source(other),
                dst_ref=target.at[here],
                send_sem=send_sem.at[d - 1],
                recv_sem=recv_sem.at[d - 1],
                device_id=(other, chan) if axis == "seq" else (mine, other),
                device_id_type=pl.DeviceIdType.MESH,
            )
        )
    for copy in copies:
        copy.start()
    return copies


def kernel(
    seq_count, chan_count,
    feat, offsets, tokens, rate_hbm, residue_hbm, skip_hbm, table_hbm, gain_hbm, weight, out_weight,
    mixed, decoded,
    held_feat, rate, residue, skip, table, gain, held, held_out,
    ut, par, own, squares, got_squares, ends_out, got_ends, proj_out, got_proj,
    pre, got_pre, carried, rows, spread, proj, dec, got_dec, mix, part, got_part,
    in_sem, w_sem, send_q, recv_q, send_e, recv_e, send_p, recv_p, send_b, recv_b,
    send_d, recv_d, send_c, recv_c,
):
    _, batch, chans, length = feat.shape
    groups = chans // LANES
    modes = rate.shape[0]
    steps = tokens.shape[1]
    count = batch * steps
    base = batch * modes
    per = max(1, groups // seq_count)
    slots = groups // per
    share = seq_count // slots
    block = modes * per
    width = gain.shape[1] * seq_count
    mine, chan = lax.axis_index("seq"), lax.axis_index("chan")

    ins = [
        pltpu.make_async_copy(source, target, in_sem.at[i])
        for i, (source, target) in enumerate(
            [(table_hbm, table), (gain_hbm, gain), (rate_hbm, rate), (residue_hbm, residue),
             (skip_hbm, skip), (feat.at[pl.ds(1, 2)], held_feat.at[pl.ds(1, 2)])]
        )
    ]
    w_copies = [pltpu.make_async_copy(weight.at[i], held.at[i], w_sem.at[i]) for i in range(3)]
    w_copies.append(pltpu.make_async_copy(feat.at[0], held_feat.at[0], w_sem.at[3]))
    w_copies.append(pltpu.make_async_copy(out_weight, held_out, w_sem.at[4]))
    for copy in ins + w_copies:
        copy.start()
    barrier = pltpu.get_barrier_semaphore()
    for d in range(1, seq_count):
        pl.semaphore_signal(
            barrier, inc=1, device_id=(lax.rem(mine + d, seq_count), chan),
            device_id_type=pl.DeviceIdType.MESH,
        )
    for d in range(1, chan_count):
        pl.semaphore_signal(
            barrier, inc=1, device_id=(mine, lax.rem(chan + d, chan_count)),
            device_id_type=pl.DeviceIdType.MESH,
        )

    vocab = table.shape[0]
    line = lax.broadcasted_iota(jnp.int32, (count, vocab), 0)
    wanted = jnp.zeros((count, vocab), jnp.int32)
    for t in range(count):
        wanted = jnp.where(line == t, tokens[t // steps, t % steps], wanted)
    hot = (wanted == lax.broadcasted_iota(jnp.int32, (count, vocab), 1)).astype(F32).astype(BF16)
    for copy in ins[:2]:
        copy.wait()
    embedded = jnp.dot(hot, table[...], preferred_element_type=F32)
    squares[...] = jnp.broadcast_to(
        jnp.sum(embedded * embedded, axis=1, keepdims=True), (count, LANES)
    )
    got_squares[mine] = squares[...]
    pl.semaphore_wait(barrier, seq_count + chan_count - 2)
    q_copies = exchange(
        mine, chan, seq_count, lambda i: squares, got_squares, send_q, recv_q
    )

    for copy in ins[2:]:
        copy.wait()
    for g in range(groups):
        lanes = slice(g * LANES, (g + 1) * LANES)
        par[pl.ds(g, modes, stride=groups), :] = rate[:, lanes]
        par[pl.ds(modes * groups + g, modes, stride=groups), :] = residue[:, lanes]
        par[2 * modes * groups + g : 2 * modes * groups + g + 1, :] = skip[:, lanes]

    place = mine * length + lax.broadcasted_iota(jnp.int32, (LANES, length), 1)

    def turn(g, carry):
        at = pl.ds(pl.multiple_of(g * LANES, LANES), LANES)
        for b in range(batch):
            product = held_feat[1, b, at, :].astype(F32) * held_feat[2, b, at, :].astype(F32)
            signal = jnp.where(place >= offsets[b], product, 0.0).astype(BF16).astype(F32)
            ut[b, pl.ds(g, length, stride=groups), :] = signal.T
        return carry

    lax.fori_loop(0, groups, turn, 0, unroll=2)

    def params(kind, h):
        first = kind * modes * groups + 8 * h
        return [par[first + m * groups : first + m * groups + 8, :] for m in range(modes)]

    for h in range(groups // 8):
        decay = [jnp.exp(-x) for x in params(0, h)]

        def end_step(t, state):
            at = pl.ds(pl.multiple_of(t * groups + 8 * h, 8), 8)
            now = [ut[b, at, :] for b in range(batch)]
            return tuple(
                decay[m] * state[b * modes + m] + now[b]
                for b in range(batch)
                for m in range(modes)
            )

        ends = lax.fori_loop(
            0, length, end_step, (jnp.zeros((8, LANES), F32),) * base, unroll=4
        )
        for r in range(base):
            for g in range(0, 8, per):
                ends_out[(8 * h + g) // per, r * per : (r + 1) * per, :] = ends[r][g : g + per]
    got_ends[mine] = ends_out[lax.div(mine, share)]
    e_copies = exchange(
        mine, chan, seq_count, lambda i: ends_out.at[lax.div(i, share)], got_ends, send_e, recv_e
    )

    for copy in q_copies:
        copy.wait()
    total = got_squares[0]
    for j in range(1, seq_count):
        total = total + got_squares[j]
    scale = lax.rsqrt(total / float(width) + 1e-05)[:, :1]
    normed = (embedded * scale * gain[...]).astype(BF16)

    def project(i):
        w_copies[i].wait()
        for c in range(0, chans, 512):
            term = jnp.dot(normed, held[i, :, c : c + 512], preferred_element_type=F32)
            for g in range(4):
                j, at = divmod(c // LANES + g, per)
                proj_out[j, pl.ds(i * count * per + at, count, stride=per), :] = term[
                    :, g * LANES : (g + 1) * LANES
                ]

    project(0)
    project(1)

    slot = lax.div(mine, share)
    for m in range(2 * modes + 1):
        own[m * per : (m + 1) * per, :] = par[pl.ds(m * groups + slot * per, per), :]
    own_rate = own[:block, :]
    power = jnp.exp(-own_rate * float(length))
    for copy in e_copies:
        copy.wait()
    final = []
    for b in range(batch):
        running = jnp.zeros((block, LANES), F32)
        for j in range(seq_count):
            pre[j, b * block : (b + 1) * block, :] = running
            running = power * running + got_ends[j, b * block : (b + 1) * block, :]
        final.append(running)
    got_pre[mine] = pre[mine]
    b_copies = exchange(mine, chan, seq_count, lambda i: pre.at[i], got_pre, send_b, recv_b)

    project(2)
    got_proj[mine] = proj_out[slot]
    p_copies = exchange(
        mine, chan, seq_count, lambda i: proj_out.at[lax.div(i, share)], got_proj, send_p, recv_p
    )

    for copy in b_copies:
        copy.wait()
    for j in range(slots):
        for r in range(base):
            carried[r, j * per : (j + 1) * per, :] = got_pre[j * share, r * per : (r + 1) * per, :]

    def convolve(h):
        decay = [jnp.exp(-x) for x in params(0, h)]
        weights = params(1, h)
        direct = par[2 * modes * groups + 8 * h : 2 * modes * groups + 8 * h + 8, :]
        for b in range(batch):

            def step(t, state):
                at = pl.ds(pl.multiple_of(t * groups + 8 * h, 8), 8)
                now = ut[b, at, :]
                state = [decay[m] * state[m] + weights[m] * now for m in range(modes)]
                terms = list(state) + [direct * now]
                while len(terms) > 1:
                    pairs = [x + y for x, y in zip(terms[::2], terms[1::2])]
                    terms = pairs + terms[len(pairs) * 2 :]
                ut[b, at, :] = terms[0]
                return tuple(state)

            begin = tuple(
                weights[m] * carried[b * modes + m, 8 * h : 8 * h + 8, :] for m in range(modes)
            )
            lax.fori_loop(0, length, step, begin, unroll=4)

    halves = groups // 8
    for h in range(halves // 2):
        convolve(h)

    for copy in p_copies:
        copy.wait()
    total = got_proj[0]
    for j in range(1, seq_count):
        total = total + got_proj[j]
    proj[...] = total.astype(BF16).astype(F32)
    own_decay = jnp.exp(-own_rate)
    own_residue = own[block : 2 * block, :]
    own_skip = own[2 * block : 2 * block + per, :]

    def projected(i, token):
        at = (i * count + token) * per
        return proj[at : at + per, :]

    for b in range(batch):
        running = final[b]
        for s in range(steps):
            token = b * steps + s
            fed = (projected(1, token) * projected(2, token)).astype(BF16).astype(F32)
            for m in range(modes):
                spread[m * per : (m + 1) * per, :] = fed
            running = own_decay * running + spread[...]
            rows[...] = own_residue * running
            value = own_skip * fed
            for m in range(modes):
                value = value + rows[m * per : (m + 1) * per, :]
            value = (projected(0, token) * value).astype(BF16).astype(F32)
            dec[token * per : (token + 1) * per, :] = value
    got_dec[mine] = dec[...]
    d_copies = exchange(mine, chan, seq_count, lambda i: dec, got_dec, send_d, recv_d)

    for h in range(halves // 2, halves):
        convolve(h)

    for copy in d_copies:
        copy.wait()
    for j in range(slots):
        for g in range(per):
            at = j * per + g
            mix[:, at * LANES : (at + 1) * LANES] = got_dec[j * share, pl.ds(g, count, stride=per), :]
    w_copies[4].wait()
    piece = held_out.shape[1] // chan_count
    decode_mix = mix[...].astype(BF16)
    for c in range(chan_count):
        part[c] = jnp.dot(
            decode_mix, held_out[:, c * piece : (c + 1) * piece], preferred_element_type=F32
        )
    got_part[chan] = part[chan]
    c_copies = exchange(
        mine, chan, chan_count, lambda i: part.at[i], got_part, send_c, recv_c, "chan"
    )

    w_copies[3].wait()

    def gate(g, carry):
        at = pl.ds(pl.multiple_of(g * LANES, LANES), LANES)
        for b in range(batch):
            value = ut[b, pl.ds(g, length, stride=groups), :].T
            mixed[b, at, :] = (held_feat[0, b, at, :].astype(F32) * value).astype(BF16)
        return carry

    lax.fori_loop(0, groups, gate, 0, unroll=2)

    for copy in c_copies:
        copy.wait()
    value = got_part[0]
    for c in range(1, chan_count):
        value = value + got_part[c]
    decoded[...] = value.astype(BF16)


def body(
    features, offsets, tokens, decay_rate, residue, skip_weight,
    embedding, norm_gain, dec_weight, out_weight,
):
    seq_count, chan_count = lax.axis_size("seq"), lax.axis_size("chan")
    _, batch, chans, length = features.shape
    modes = decay_rate.shape[0]
    steps = tokens.shape[1]
    count = batch * steps
    groups = chans // LANES
    per = max(1, groups // seq_count)
    slots = groups // per
    base = batch * modes
    out_width = out_weight.shape[1]
    piece = out_width // chan_count

    def wide(*shape):
        return pltpu.VMEM(shape, F32)

    def sems(number):
        return pltpu.SemaphoreType.DMA((number,))

    mixed, decoded = pl.pallas_call(
        functools.partial(kernel, seq_count, chan_count),
        out_shape=(
            jax.ShapeDtypeStruct((batch, chans, length), BF16),
            jax.ShapeDtypeStruct((count, piece), BF16),
        ),
        in_specs=[ANY, SMEM, SMEM, ANY, ANY, ANY, ANY, ANY, ANY, ANY],
        out_specs=(VMEM, VMEM),
        scratch_shapes=[
            pltpu.VMEM(features.shape, BF16),
            wide(modes, chans),
            wide(modes, chans),
            wide(1, chans),
            pltpu.VMEM(embedding.shape, BF16),
            wide(1, norm_gain.shape[0]),
            pltpu.VMEM(dec_weight.shape, BF16),
            pltpu.VMEM(out_weight.shape, BF16),
            wide(batch, length * groups, LANES),
            wide((2 * modes + 1) * groups, LANES),
            wide((2 * modes + 1) * per, LANES),
            wide(count, LANES),
            wide(seq_count, count, LANES),
            wide(slots, base * per, LANES),
            wide(seq_count, base * per, LANES),
            wide(slots, 3 * count * per, LANES),
            wide(seq_count, 3 * count * per, LANES),
            wide(seq_count, base * per, LANES),
            wide(seq_count, base * per, LANES),
            wide(base, groups, LANES),
            wide(modes * per, LANES),
            wide(modes * per, LANES),
            wide(3 * count * per, LANES),
            wide(count * per, LANES),
            wide(seq_count, count * per, LANES),
            wide(count, chans),
            wide(chan_count, count, piece),
            wide(chan_count, count, piece),
            sems(6),
            sems(5),
        ]
        + [sems(seq_count - 1)] * 10
        + [sems(chan_count - 1)] * 2,
        compiler_params=pltpu.CompilerParams(
            vmem_limit_bytes=LIMIT, collective_id=0, has_side_effects=True
        ),
        name="layer",
    )(
        features, offsets, tokens, decay_rate, residue, skip_weight[None],
        embedding, norm_gain[None], dec_weight, out_weight,
    )
    return mixed, decoded.reshape(batch, steps, -1)


def solution(mesh):
    placed = (
        P(None, None, "chan", "seq"),
        P(),
        P(),
        P(None, "chan"),
        P(None, "chan"),
        P("chan"),
        P(None, "seq"),
        P("seq"),
        P(None, "seq", "chan"),
        P("chan", "seq"),
    )
    return jax.shard_map(
        body,
        mesh=mesh,
        in_specs=placed,
        out_specs=(P(None, "chan", "seq"), P(None, None, ("seq", "chan"))),
        check_vma=False,
    )
```

```python
import functools

import jax
import jax.numpy as jnp
from jax import lax
from jax.experimental import pallas as pl
from jax.experimental.pallas import tpu as pltpu
from jax.sharding import PartitionSpec as P

LANES = 128
F32 = jnp.float32
BF16 = jnp.bfloat16
VMEM = pl.BlockSpec(memory_space=pltpu.VMEM)
ANY = pl.BlockSpec(memory_space=pl.ANY)
SMEM = pl.BlockSpec(memory_space=pltpu.SMEM)
LIMIT = 56 * 2**20


def exchange(mine, chan, count, source, target, send_sem, recv_sem, axis="seq"):
    here = mine if axis == "seq" else chan
    copies = []
    for d in range(1, count):
        other = lax.rem(here + d, count)
        copies.append(
            pltpu.make_async_remote_copy(
                src_ref=source(other),
                dst_ref=target.at[here],
                send_sem=send_sem.at[d - 1],
                recv_sem=recv_sem.at[d - 1],
                device_id=(other, chan) if axis == "seq" else (mine, other),
                device_id_type=pl.DeviceIdType.MESH,
            )
        )
    for copy in copies:
        copy.start()
    return copies


def kernel(
    seq_count, chan_count,
    feat, offsets, tokens, rate_hbm, residue_hbm, skip_hbm, table_hbm, gain_hbm, weight, out_weight,
    conv, decoded,
    held_feat, rate, residue, skip, table, gain, held, held_out,
    ut, par, own, squares, got_squares, ends_out, got_ends, proj_out, got_proj,
    pre, got_pre, carried, rows, spread, proj, dec, got_dec, mix, part, got_part,
    in_sem, w_sem, out_sem, send_q, recv_q, send_e, recv_e, send_p, recv_p, send_b, recv_b,
    send_d, recv_d, send_c, recv_c,
):
    _, batch, chans, length = feat.shape
    groups = chans // LANES
    modes = rate.shape[0]
    steps = tokens.shape[1]
    count = batch * steps
    base = batch * modes
    per = max(1, groups // seq_count)
    slots = groups // per
    share = seq_count // slots
    block = modes * per
    width = gain.shape[1] * seq_count
    mine, chan = lax.axis_index("seq"), lax.axis_index("chan")

    ins = [
        pltpu.make_async_copy(source, target, in_sem.at[i])
        for i, (source, target) in enumerate(
            [(table_hbm, table), (gain_hbm, gain), (rate_hbm, rate), (residue_hbm, residue),
             (skip_hbm, skip), (feat.at[pl.ds(1, 2)], held_feat)]
        )
    ]
    w_copies = [pltpu.make_async_copy(weight.at[i], held.at[i], w_sem.at[i]) for i in range(3)]
    w_copies.append(pltpu.make_async_copy(out_weight, held_out, w_sem.at[3]))
    for copy in ins + w_copies:
        copy.start()
    barrier = pltpu.get_barrier_semaphore()
    for d in range(1, seq_count):
        pl.semaphore_signal(
            barrier, inc=1, device_id=(lax.rem(mine + d, seq_count), chan),
            device_id_type=pl.DeviceIdType.MESH,
        )
    for d in range(1, chan_count):
        pl.semaphore_signal(
            barrier, inc=1, device_id=(mine, lax.rem(chan + d, chan_count)),
            device_id_type=pl.DeviceIdType.MESH,
        )

    vocab = table.shape[0]
    line = lax.broadcasted_iota(jnp.int32, (count, vocab), 0)
    wanted = jnp.zeros((count, vocab), jnp.int32)
    for t in range(count):
        wanted = jnp.where(line == t, tokens[t // steps, t % steps], wanted)
    hot = (wanted == lax.broadcasted_iota(jnp.int32, (count, vocab), 1)).astype(F32).astype(BF16)
    for copy in ins[:2]:
        copy.wait()
    embedded = jnp.dot(hot, table[...], preferred_element_type=F32)
    squares[...] = jnp.broadcast_to(
        jnp.sum(embedded * embedded, axis=1, keepdims=True), (count, LANES)
    )
    got_squares[mine] = squares[...]
    pl.semaphore_wait(barrier, seq_count + chan_count - 2)
    q_copies = exchange(
        mine, chan, seq_count, lambda i: squares, got_squares, send_q, recv_q
    )

    for copy in ins[2:]:
        copy.wait()
    for g in range(groups):
        lanes = slice(g * LANES, (g + 1) * LANES)
        par[pl.ds(g, modes, stride=groups), :] = rate[:, lanes]
        par[pl.ds(modes * groups + g, modes, stride=groups), :] = residue[:, lanes]
        par[2 * modes * groups + g : 2 * modes * groups + g + 1, :] = skip[:, lanes]

    place = mine * length + lax.broadcasted_iota(jnp.int32, (LANES, length), 1)

    def turn(g, carry):
        at = pl.ds(pl.multiple_of(g * LANES, LANES), LANES)
        for b in range(batch):
            product = held_feat[0, b, at, :].astype(F32) * held_feat[1, b, at, :].astype(F32)
            signal = jnp.where(place >= offsets[b], product, 0.0).astype(BF16).astype(F32)
            ut[b, pl.ds(g, length, stride=groups), :] = signal.T
        return carry

    lax.fori_loop(0, groups, turn, 0, unroll=2)

    def params(kind, h):
        first = kind * modes * groups + 8 * h
        return [par[first + m * groups : first + m * groups + 8, :] for m in range(modes)]

    def project(i, chunk):
        columns = pl.ds(pl.multiple_of(chunk * 2 * LANES, 2 * LANES), 2 * LANES)
        term = jnp.dot(normed, held[i, :, columns], preferred_element_type=F32)
        for g in range(2):
            j, at = chunk * (2 // per) + g // per, g % per
            proj_out[j, pl.ds(i * count * per + at, count, stride=per), :] = term[
                :, g * LANES : (g + 1) * LANES
            ]

    chunks = groups // 2
    halves = groups // 8
    for h in range(halves):
        if h == halves - 1:
            for copy in q_copies:
                copy.wait()
            total = got_squares[0]
            for j in range(1, seq_count):
                total = total + got_squares[j]
            scale = lax.rsqrt(total / float(width) + 1e-05)[:, :1]
            normed = (embedded * scale * gain[...]).astype(BF16)
            w_copies[0].wait()
        decay = [jnp.exp(-x) for x in params(0, h)]
        zero = jnp.zeros((8, LANES), F32)

        def end_step(t, state):
            at = pl.ds(pl.multiple_of(t * groups + 8 * h, 8), 8)
            now = [ut[b, at, :] for b in range(batch)]
            return tuple(
                decay[m] * state[b * modes + m] + now[b]
                for b in range(batch)
                for m in range(modes)
            )

        def end_steps(chunk, state):
            project(0, chunk)
            for t in range(length // chunks):
                state = end_step(chunk * (length // chunks) + t, state)
            return state

        if h == halves - 1:
            ends = lax.fori_loop(0, chunks, end_steps, (zero,) * base)
        else:
            ends = lax.fori_loop(0, length, end_step, (zero,) * base, unroll=4)
        for r in range(base):
            for g in range(0, 8, per):
                ends_out[(8 * h + g) // per, r * per : (r + 1) * per, :] = ends[r][g : g + per]
    got_ends[mine] = ends_out[lax.div(mine, share)]
    e_copies = exchange(
        mine, chan, seq_count, lambda i: ends_out.at[lax.div(i, share)], got_ends, send_e, recv_e
    )

    w_copies[1].wait()
    for chunk in range(chunks):
        project(1, chunk)

    slot = lax.div(mine, share)
    for m in range(2 * modes + 1):
        own[m * per : (m + 1) * per, :] = par[pl.ds(m * groups + slot * per, per), :]
    own_rate = own[:block, :]
    power = jnp.exp(-own_rate * float(length))
    for copy in e_copies:
        copy.wait()
    final = []
    for b in range(batch):
        running = jnp.zeros((block, LANES), F32)
        for j in range(seq_count):
            pre[j, b * block : (b + 1) * block, :] = running
            running = power * running + got_ends[j, b * block : (b + 1) * block, :]
        final.append(running)
    got_pre[mine] = pre[mine]
    b_copies = exchange(mine, chan, seq_count, lambda i: pre.at[i], got_pre, send_b, recv_b)

    w_copies[2].wait()
    for chunk in range(chunks):
        project(2, chunk)
    got_proj[mine] = proj_out[slot]
    p_copies = exchange(
        mine, chan, seq_count, lambda i: proj_out.at[lax.div(i, share)], got_proj, send_p, recv_p
    )

    for copy in b_copies:
        copy.wait()
    for j in range(slots):
        for r in range(base):
            carried[r, j * per : (j + 1) * per, :] = got_pre[j * share, r * per : (r + 1) * per, :]

    def convolve(b, h):
        decay = [jnp.exp(-x) for x in params(0, h)]
        weights = params(1, h)
        direct = par[2 * modes * groups + 8 * h : 2 * modes * groups + 8 * h + 8, :]

        def step(t, state):
            at = pl.ds(pl.multiple_of(t * groups + 8 * h, 8), 8)
            now = ut[b, at, :]
            state = [decay[m] * state[m] + weights[m] * now for m in range(modes)]
            terms = list(state) + [direct * now]
            while len(terms) > 1:
                pairs = [x + y for x, y in zip(terms[::2], terms[1::2])]
                terms = pairs + terms[len(pairs) * 2 :]
            ut[b, at, :] = terms[0]
            return tuple(state)

        begin = tuple(
            weights[m] * carried[b * modes + m, 8 * h : 8 * h + 8, :] for m in range(modes)
        )
        lax.fori_loop(0, length, step, begin, unroll=4)

    units = [(b, h) for b in range(batch) for h in range(halves)]
    conv_copies = [pltpu.make_async_copy(ut.at[b], conv.at[b], out_sem.at[b]) for b in range(batch)]

    def run(first, stop):
        for b, h in units[first:stop]:
            convolve(b, h)
            if h == halves - 1:
                conv_copies[b].start()

    run(0, 1)

    for copy in p_copies:
        copy.wait()
    total = got_proj[0]
    for j in range(1, seq_count):
        total = total + got_proj[j]
    proj[...] = total.astype(BF16).astype(F32)
    own_decay = jnp.exp(-own_rate)
    own_residue = own[block : 2 * block, :]
    own_skip = own[2 * block : 2 * block + per, :]

    def projected(i, token):
        at = (i * count + token) * per
        return proj[at : at + per, :]

    for b in range(batch):
        running = final[b]
        for s in range(steps):
            token = b * steps + s
            fed = (projected(1, token) * projected(2, token)).astype(BF16).astype(F32)
            for m in range(modes):
                spread[m * per : (m + 1) * per, :] = fed
            running = own_decay * running + spread[...]
            rows[...] = own_residue * running
            value = own_skip * fed
            for m in range(modes):
                value = value + rows[m * per : (m + 1) * per, :]
            value = (projected(0, token) * value).astype(BF16).astype(F32)
            dec[token * per : (token + 1) * per, :] = value
    got_dec[mine] = dec[...]
    d_copies = exchange(mine, chan, seq_count, lambda i: dec, got_dec, send_d, recv_d)

    run(1, len(units) - 1)

    for copy in d_copies:
        copy.wait()
    for j in range(slots):
        for g in range(per):
            at = j * per + g
            mix[:, at * LANES : (at + 1) * LANES] = got_dec[j * share, pl.ds(g, count, stride=per), :]
    w_copies[3].wait()
    piece = held_out.shape[1] // chan_count
    decode_mix = mix[...].astype(BF16)
    for c in range(chan_count):
        part[c] = jnp.dot(
            decode_mix, held_out[:, c * piece : (c + 1) * piece], preferred_element_type=F32
        )
    got_part[chan] = part[chan]
    c_copies = exchange(
        mine, chan, chan_count, lambda i: part.at[i], got_part, send_c, recv_c, "chan"
    )

    run(len(units) - 1, len(units))
    for copy in c_copies:
        copy.wait()
    value = got_part[0]
    for c in range(1, chan_count):
        value = value + got_part[c]
    value = value.astype(BF16)
    for b in range(batch):
        decoded[b] = value[b * steps : (b + 1) * steps]
    for copy in conv_copies:
        copy.wait()


def gate(query, conv, mixed):
    _, _, chans, length = query.shape
    groups = chans // LANES

    def turn(g, carry):
        at = pl.ds(pl.multiple_of(g * LANES, LANES), LANES)
        value = conv[0, pl.ds(g, length, stride=groups), :].T
        mixed[0, at, :] = (query[0, 0, at, :].astype(F32) * value).astype(BF16)
        return carry

    lax.fori_loop(0, groups, turn, 0, unroll=4)


def body(
    features, offsets, tokens, decay_rate, residue, skip_weight,
    embedding, norm_gain, dec_weight, out_weight,
):
    seq_count, chan_count = lax.axis_size("seq"), lax.axis_size("chan")
    _, batch, chans, length = features.shape
    modes = decay_rate.shape[0]
    steps = tokens.shape[1]
    count = batch * steps
    groups = chans // LANES
    per = max(1, groups // seq_count)
    slots = groups // per
    base = batch * modes
    out_width = out_weight.shape[1]
    piece = out_width // chan_count

    def wide(*shape):
        return pltpu.VMEM(shape, F32)

    def sems(number):
        return pltpu.SemaphoreType.DMA((number,))

    conv, decoded = pl.pallas_call(
        functools.partial(kernel, seq_count, chan_count),
        out_shape=(
            jax.ShapeDtypeStruct((batch, length * groups, LANES), F32),
            jax.ShapeDtypeStruct((batch, steps, piece), BF16),
        ),
        in_specs=[ANY, SMEM, SMEM, ANY, ANY, ANY, ANY, ANY, ANY, ANY],
        out_specs=(ANY, VMEM),
        scratch_shapes=[
            pltpu.VMEM((2,) + features.shape[1:], BF16),
            wide(modes, chans),
            wide(modes, chans),
            wide(1, chans),
            pltpu.VMEM(embedding.shape, BF16),
            wide(1, norm_gain.shape[0]),
            pltpu.VMEM(dec_weight.shape, BF16),
            pltpu.VMEM(out_weight.shape, BF16),
            wide(batch, length * groups, LANES),
            wide((2 * modes + 1) * groups, LANES),
            wide((2 * modes + 1) * per, LANES),
            wide(count, LANES),
            wide(seq_count, count, LANES),
            wide(slots, base * per, LANES),
            wide(seq_count, base * per, LANES),
            wide(slots, 3 * count * per, LANES),
            wide(seq_count, 3 * count * per, LANES),
            wide(seq_count, base * per, LANES),
            wide(seq_count, base * per, LANES),
            wide(base, groups, LANES),
            wide(modes * per, LANES),
            wide(modes * per, LANES),
            wide(3 * count * per, LANES),
            wide(count * per, LANES),
            wide(seq_count, count * per, LANES),
            wide(count, chans),
            wide(chan_count, count, piece),
            wide(chan_count, count, piece),
            sems(6),
            sems(4),
            sems(batch),
        ]
        + [sems(seq_count - 1)] * 10
        + [sems(chan_count - 1)] * 2,
        compiler_params=pltpu.CompilerParams(
            vmem_limit_bytes=LIMIT, collective_id=0, has_side_effects=True
        ),
        name="layer",
    )(
        features, offsets, tokens, decay_rate, residue, skip_weight[None],
        embedding, norm_gain[None], dec_weight, out_weight,
    )
    mixed = pl.pallas_call(
        gate,
        grid=(batch,),
        out_shape=jax.ShapeDtypeStruct((batch, chans, length), BF16),
        in_specs=[
            pl.BlockSpec((1, 1, chans, length), lambda b: (0, b, 0, 0)),
            pl.BlockSpec((1, length * groups, LANES), lambda b: (b, 0, 0)),
        ],
        out_specs=pl.BlockSpec((1, chans, length), lambda b: (b, 0, 0)),
        compiler_params=pltpu.CompilerParams(vmem_limit_bytes=LIMIT),
        name="gate",
    )(features, conv)
    return mixed, decoded


def solution(mesh):
    placed = (
        P(None, None, "chan", "seq"),
        P(),
        P(),
        P(None, "chan"),
        P(None, "chan"),
        P("chan"),
        P(None, "seq"),
        P("seq"),
        P(None, "seq", "chan"),
        P("chan", "seq"),
    )
    return jax.shard_map(
        body,
        mesh=mesh,
        in_specs=placed,
        out_specs=(P(None, "chan", "seq"), P(None, None, ("seq", "chan"))),
        check_vma=False,
    )
```

```python
import functools

import jax
import jax.numpy as jnp
from jax import lax
from jax.experimental import pallas as pl
from jax.experimental.pallas import tpu as pltpu
from jax.sharding import PartitionSpec as P

LANES = 128
F32 = jnp.float32
BF16 = jnp.bfloat16
VMEM = pl.BlockSpec(memory_space=pltpu.VMEM)
ANY = pl.BlockSpec(memory_space=pl.ANY)
SMEM = pl.BlockSpec(memory_space=pltpu.SMEM)
LIMIT = 56 * 2**20


def exchange(mine, chan, count, source, target, send_sem, recv_sem, axis="seq", part=None):
    here = mine if axis == "seq" else chan
    first = 0 if part is None else part[0] * (count - 1)
    copies = []
    for d in range(1, count):
        other = lax.rem(here + d, count)
        copies.append(
            pltpu.make_async_remote_copy(
                src_ref=source(other),
                dst_ref=target.at[here] if part is None else target.at[here, pl.ds(*part[1:])],
                send_sem=send_sem.at[first + d - 1],
                recv_sem=recv_sem.at[first + d - 1],
                device_id=(other, chan) if axis == "seq" else (mine, other),
                device_id_type=pl.DeviceIdType.MESH,
            )
        )
    for copy in copies:
        copy.start()
    return copies


def kernel(
    seq_count, chan_count,
    feat, offsets, tokens, rate_hbm, residue_hbm, skip_hbm, table_hbm, gain_hbm, weight, out_weight,
    mixed, decoded,
    held_feat, rate, residue, skip, table, gain, held, held_out,
    ut, par, own, squares, got_squares, ends_out, got_ends, proj_out, got_proj,
    pre, got_pre, carried, rows, spread, proj, dec, got_dec, mix, part, got_part,
    in_sem, w_sem, send_q, recv_q, send_e, recv_e, send_p, recv_p, send_b, recv_b,
    send_d, recv_d, send_c, recv_c,
):
    _, batch, chans, length = feat.shape
    groups = chans // LANES
    modes = rate.shape[0]
    steps = tokens.shape[1]
    count = batch * steps
    base = batch * modes
    per = max(1, groups // seq_count)
    slots = groups // per
    share = seq_count // slots
    block = modes * per
    width = gain.shape[1] * seq_count
    mine, chan = lax.axis_index("seq"), lax.axis_index("chan")

    ins = [
        pltpu.make_async_copy(source, target, in_sem.at[i])
        for i, (source, target) in enumerate(
            [(table_hbm, table), (gain_hbm, gain), (rate_hbm, rate), (residue_hbm, residue),
             (skip_hbm, skip), (feat.at[pl.ds(1, 2)], held_feat.at[pl.ds(1, 2)])]
        )
    ]
    w_copies = [pltpu.make_async_copy(weight.at[i], held.at[i], w_sem.at[i]) for i in range(3)]
    w_copies.append(pltpu.make_async_copy(feat.at[0], held_feat.at[0], w_sem.at[3]))
    w_copies.append(pltpu.make_async_copy(out_weight, held_out, w_sem.at[4]))
    for copy in ins + w_copies:
        copy.start()
    barrier = pltpu.get_barrier_semaphore()
    for d in range(1, seq_count):
        pl.semaphore_signal(
            barrier, inc=1, device_id=(lax.rem(mine + d, seq_count), chan),
            device_id_type=pl.DeviceIdType.MESH,
        )
    for d in range(1, chan_count):
        pl.semaphore_signal(
            barrier, inc=1, device_id=(mine, lax.rem(chan + d, chan_count)),
            device_id_type=pl.DeviceIdType.MESH,
        )

    vocab = table.shape[0]
    line = lax.broadcasted_iota(jnp.int32, (count, vocab), 0)
    wanted = jnp.zeros((count, vocab), jnp.int32)
    for t in range(count):
        wanted = jnp.where(line == t, tokens[t // steps, t % steps], wanted)
    hot = (wanted == lax.broadcasted_iota(jnp.int32, (count, vocab), 1)).astype(F32).astype(BF16)
    for copy in ins[:2]:
        copy.wait()
    embedded = jnp.dot(hot, table[...], preferred_element_type=F32)
    squares[...] = jnp.broadcast_to(
        jnp.sum(embedded * embedded, axis=1, keepdims=True), (count, LANES)
    )
    got_squares[mine] = squares[...]
    pl.semaphore_wait(barrier, seq_count + chan_count - 2)
    q_copies = exchange(
        mine, chan, seq_count, lambda i: squares, got_squares, send_q, recv_q
    )

    for copy in ins[2:]:
        copy.wait()
    for g in range(groups):
        lanes = slice(g * LANES, (g + 1) * LANES)
        par[pl.ds(g, modes, stride=groups), :] = rate[:, lanes]
        par[pl.ds(modes * groups + g, modes, stride=groups), :] = residue[:, lanes]
        par[2 * modes * groups + g : 2 * modes * groups + g + 1, :] = skip[:, lanes]

    place = mine * length + lax.broadcasted_iota(jnp.int32, (LANES, length), 1)

    def turn(g, carry):
        at = pl.ds(pl.multiple_of(g * LANES, LANES), LANES)
        for b in range(batch):
            product = held_feat[1, b, at, :].astype(F32) * held_feat[2, b, at, :].astype(F32)
            signal = jnp.where(place >= offsets[b], product, 0.0).astype(BF16).astype(F32)
            ut[b, pl.ds(g, length, stride=groups), :] = signal.T
        return carry

    lax.fori_loop(0, groups, turn, 0, unroll=2)

    def params(kind, h):
        first = kind * modes * groups + 8 * h
        return [par[first + m * groups : first + m * groups + 8, :] for m in range(modes)]

    def part_of(b):
        return (b, b * block, block)

    e_copies = []
    for b in range(batch):
        for h in range(groups // 8):
            decay = [jnp.exp(-x) for x in params(0, h)]

            def end_step(t, state):
                now = ut[b, pl.ds(pl.multiple_of(t * groups + 8 * h, 8), 8), :]
                return tuple(decay[m] * state[m] + now for m in range(modes))

            ends = lax.fori_loop(
                0, length, end_step, (jnp.zeros((8, LANES), F32),) * modes, unroll=8
            )
            for m in range(modes):
                r = b * modes + m
                for g in range(0, 8, per):
                    ends_out[(8 * h + g) // per, r * per : (r + 1) * per, :] = ends[m][g : g + per]
        rows_of = pl.ds(b * block, block)
        got_ends[mine, rows_of, :] = ends_out[lax.div(mine, share), rows_of, :]
        e_copies.append(exchange(
            mine, chan, seq_count, lambda i: ends_out.at[lax.div(i, share), rows_of], got_ends,
            send_e, recv_e, part=part_of(b),
        ))

    for copy in q_copies:
        copy.wait()
    total = got_squares[0]
    for j in range(1, seq_count):
        total = total + got_squares[j]
    scale = lax.rsqrt(total / float(width) + 1e-05)[:, :1]
    normed = (embedded * scale * gain[...]).astype(BF16)

    def project(i):
        w_copies[i].wait()
        for c in range(0, chans, 512):
            term = jnp.dot(normed, held[i, :, c : c + 512], preferred_element_type=F32)
            for g in range(4):
                j, at = divmod(c // LANES + g, per)
                proj_out[j, pl.ds(i * count * per + at, count, stride=per), :] = term[
                    :, g * LANES : (g + 1) * LANES
                ]

    project(0)

    slot = lax.div(mine, share)
    for m in range(2 * modes + 1):
        own[m * per : (m + 1) * per, :] = par[pl.ds(m * groups + slot * per, per), :]
    own_rate = own[:block, :]
    power = jnp.exp(-own_rate * float(length))
    final, b_copies = [], []
    for b in range(batch):
        for copy in e_copies[b]:
            copy.wait()
        running = jnp.zeros((block, LANES), F32)
        rows_of = pl.ds(b * block, block)
        for j in range(seq_count):
            pre[j, b * block : (b + 1) * block, :] = running
            running = power * running + got_ends[j, b * block : (b + 1) * block, :]
        final.append(running)
        got_pre[mine, rows_of, :] = pre[mine, rows_of, :]
        b_copies.append(exchange(
            mine, chan, seq_count, lambda i: pre.at[i, rows_of], got_pre,
            send_b, recv_b, part=part_of(b),
        ))
        if b == 0:
            project(1)
    project(2)
    got_proj[mine] = proj_out[slot]
    p_copies = exchange(
        mine, chan, seq_count, lambda i: proj_out.at[lax.div(i, share)], got_proj, send_p, recv_p
    )

    def convolve(b):
        for copy in b_copies[b]:
            copy.wait()
        for j in range(slots):
            for r in range(b * modes, (b + 1) * modes):
                carried[r, j * per : (j + 1) * per, :] = got_pre[
                    j * share, r * per : (r + 1) * per, :
                ]
        for h in range(groups // 8):
            decay = [jnp.exp(-x) for x in params(0, h)]
            weights = params(1, h)
            direct = par[2 * modes * groups + 8 * h : 2 * modes * groups + 8 * h + 8, :]

            def step(t, state):
                at = pl.ds(pl.multiple_of(t * groups + 8 * h, 8), 8)
                now = ut[b, at, :]
                state = [decay[m] * state[m] + weights[m] * now for m in range(modes)]
                terms = list(state) + [direct * now]
                while len(terms) > 1:
                    pairs = [x + y for x, y in zip(terms[::2], terms[1::2])]
                    terms = pairs + terms[len(pairs) * 2 :]
                ut[b, at, :] = terms[0]
                return tuple(state)

            begin = tuple(
                weights[m] * carried[b * modes + m, 8 * h : 8 * h + 8, :] for m in range(modes)
            )
            lax.fori_loop(0, length, step, begin, unroll=4)

    for b in range(batch - batch // 2):
        convolve(b)

    for copy in p_copies:
        copy.wait()
    total = got_proj[0]
    for j in range(1, seq_count):
        total = total + got_proj[j]
    proj[...] = total.astype(BF16).astype(F32)
    own_decay = jnp.exp(-own_rate)
    own_residue = own[block : 2 * block, :]
    own_skip = own[2 * block : 2 * block + per, :]

    def projected(i, token):
        at = (i * count + token) * per
        return proj[at : at + per, :]

    for b in range(batch):
        running = final[b]
        for s in range(steps):
            token = b * steps + s
            fed = (projected(1, token) * projected(2, token)).astype(BF16).astype(F32)
            for m in range(modes):
                spread[m * per : (m + 1) * per, :] = fed
            running = own_decay * running + spread[...]
            rows[...] = own_residue * running
            value = own_skip * fed
            for m in range(modes):
                value = value + rows[m * per : (m + 1) * per, :]
            value = (projected(0, token) * value).astype(BF16).astype(F32)
            dec[token * per : (token + 1) * per, :] = value
    got_dec[mine] = dec[...]
    d_copies = exchange(mine, chan, seq_count, lambda i: dec, got_dec, send_d, recv_d)

    for b in range(batch - batch // 2, batch):
        convolve(b)

    for copy in d_copies:
        copy.wait()
    for j in range(slots):
        for g in range(per):
            at = j * per + g
            mix[:, at * LANES : (at + 1) * LANES] = got_dec[j * share, pl.ds(g, count, stride=per), :]
    w_copies[4].wait()
    piece = held_out.shape[1] // chan_count
    decode_mix = mix[...].astype(BF16)
    for c in range(chan_count):
        part[c] = jnp.dot(
            decode_mix, held_out[:, c * piece : (c + 1) * piece], preferred_element_type=F32
        )
    got_part[chan] = part[chan]
    c_copies = exchange(
        mine, chan, chan_count, lambda i: part.at[i], got_part, send_c, recv_c, "chan"
    )

    w_copies[3].wait()

    def gate(g, carry):
        at = pl.ds(pl.multiple_of(g * LANES, LANES), LANES)
        for b in range(batch):
            value = ut[b, pl.ds(g, length, stride=groups), :].T
            mixed[b, at, :] = (held_feat[0, b, at, :].astype(F32) * value).astype(BF16)
        return carry

    lax.fori_loop(0, groups, gate, 0, unroll=2)

    for copy in c_copies:
        copy.wait()
    value = got_part[0]
    for c in range(1, chan_count):
        value = value + got_part[c]
    value = value.astype(BF16)
    for b in range(batch):
        decoded[b] = value[b * steps : (b + 1) * steps]


def body(
    features, offsets, tokens, decay_rate, residue, skip_weight,
    embedding, norm_gain, dec_weight, out_weight,
):
    seq_count, chan_count = lax.axis_size("seq"), lax.axis_size("chan")
    _, batch, chans, length = features.shape
    modes = decay_rate.shape[0]
    steps = tokens.shape[1]
    count = batch * steps
    groups = chans // LANES
    per = max(1, groups // seq_count)
    slots = groups // per
    base = batch * modes
    out_width = out_weight.shape[1]
    piece = out_width // chan_count

    def wide(*shape):
        return pltpu.VMEM(shape, F32)

    def sems(number):
        return pltpu.SemaphoreType.DMA((number,))

    mixed, decoded = pl.pallas_call(
        functools.partial(kernel, seq_count, chan_count),
        out_shape=(
            jax.ShapeDtypeStruct((batch, chans, length), BF16),
            jax.ShapeDtypeStruct((batch, steps, piece), BF16),
        ),
        in_specs=[ANY, SMEM, SMEM, ANY, ANY, ANY, ANY, ANY, ANY, ANY],
        out_specs=(VMEM, VMEM),
        scratch_shapes=[
            pltpu.VMEM(features.shape, BF16),
            wide(modes, chans),
            wide(modes, chans),
            wide(1, chans),
            pltpu.VMEM(embedding.shape, BF16),
            wide(1, norm_gain.shape[0]),
            pltpu.VMEM(dec_weight.shape, BF16),
            pltpu.VMEM(out_weight.shape, BF16),
            wide(batch, length * groups, LANES),
            wide((2 * modes + 1) * groups, LANES),
            wide((2 * modes + 1) * per, LANES),
            wide(count, LANES),
            wide(seq_count, count, LANES),
            wide(slots, base * per, LANES),
            wide(seq_count, base * per, LANES),
            wide(slots, 3 * count * per, LANES),
            wide(seq_count, 3 * count * per, LANES),
            wide(seq_count, base * per, LANES),
            wide(seq_count, base * per, LANES),
            wide(base, groups, LANES),
            wide(modes * per, LANES),
            wide(modes * per, LANES),
            wide(3 * count * per, LANES),
            wide(count * per, LANES),
            wide(seq_count, count * per, LANES),
            wide(count, chans),
            wide(chan_count, count, piece),
            wide(chan_count, count, piece),
            sems(6),
            sems(5),
        ]
        + [sems(seq_count - 1)] * 2
        + [sems(batch * (seq_count - 1))] * 2
        + [sems(seq_count - 1)] * 2
        + [sems(batch * (seq_count - 1))] * 2
        + [sems(seq_count - 1)] * 2
        + [sems(chan_count - 1)] * 2,
        compiler_params=pltpu.CompilerParams(
            vmem_limit_bytes=LIMIT, collective_id=0, has_side_effects=True
        ),
        name="layer",
    )(
        features, offsets, tokens, decay_rate, residue, skip_weight[None],
        embedding, norm_gain[None], dec_weight, out_weight,
    )
    return mixed, decoded


def solution(mesh):
    placed = (
        P(None, None, "chan", "seq"),
        P(),
        P(),
        P(None, "chan"),
        P(None, "chan"),
        P("chan"),
        P(None, "seq"),
        P("seq"),
        P(None, "seq", "chan"),
        P("chan", "seq"),
    )
    return jax.shard_map(
        body,
        mesh=mesh,
        in_specs=placed,
        out_specs=(P(None, "chan", "seq"), P(None, None, ("seq", "chan"))),
        check_vma=False,
    )
```
